32 devices in a mesh: lon: 8 (over y, x, core), lat: 4 (over z).
Axes of the slice: x: 2, y: 2, z: 4, core: 2. Of those that a mesh axis runs over, the one named last changes fastest.
Arguments:
- grad_field: float32 [16, 32, 137, 128], P('lat', 'lon'), may hold values from -6 to 6
- lat_weights: float32 [8, 3], replicated, may hold values from 0.2 to 1
- block_offsets: int32 [8, 5], replicated, may hold values from -3 to 3, as said below
- filters: bfloat16 [8, 5, 128, 128], replicated, may hold values from -0.25 to 0.25
- vertical: bfloat16 [8, 137, 137], replicated, may hold values from -0.5 to 0.5
- slot_of_band: int32 [8], replicated, may hold values from 0 to 7, each once
Outputs:
- band_control: bfloat16 [8, 16, 32, 137, 128], P('lat', 'lon')
The draws below stay inside these ranges and needn't reach their ends.
Inputs may be any that keep to these rules, and one draw needn't show every extreme that they name: `block_offsets`: each band names 5 different offsets; offset -3 is named by some band and offset 3 by some band.
All inputs are finite; a program needn't handle non-finite values.
Results may differ from the reference program's by a relative error of at most 0.0058.
Values may be sent and summed in bfloat16 or wider, within the bound.
No kernel may reach another device: no remote copies, remote signals or barrier semaphores. Data moves between devices by JAX's collectives and lax.ppermute only.
A program may use at most 128 MiB of HBM per device.

```python
import jax
import jax.numpy as jnp
from jax import lax

LEV = 137
BLOCK = 128
NB = 8
KB = 5
REACH = 3
NLAT = 16
NLON = 4096


def draw_block_offsets(key, part):
    choices_count = 2 * REACH + 1

    def one_row(row_key):
        return jax.random.permutation(row_key, choices_count).astype(jnp.int32)
    scores = jax.vmap(one_row)(jax.random.split(jax.random.fold_in(key, 17), NB))
    scores = scores.at[0, 0].add(100).at[1, choices_count - 1].add(100)
    picked = lax.top_k(scores, KB)[1]
    return (picked - REACH).astype(jnp.int32)


def levels(stream_key, shape, pieces, smallest, largest):
    factor_of = 1.0
    for dim, blocks in pieces:
        steps = jax.random.uniform(jax.random.fold_in(jax.random.fold_in(stream_key, 6), dim), (blocks,), jnp.float32, smallest / len(pieces), largest / len(pieces))
        factor_of = factor_of * jnp.repeat(jnp.exp(steps), shape[dim] // blocks).reshape((-1,) + (1,) * (len(shape) - 1 - dim))
    return factor_of


def gaussian(key, dims, deviation, reach, cuts=(), held_as=jnp.bfloat16):
    factor_of = levels(key, dims, cuts, -0.22, 0.18) if cuts else 1.0
    entries = jax.random.normal(key, dims, jnp.float32) * deviation * factor_of
    return jnp.minimum(jnp.maximum(entries, -reach), reach).astype(held_as)


def setup_inputs(seed: int = 0) -> dict:
    arg_keys = jax.random.split(jax.random.key(seed), 7)
    return {
        "grad_field": gaussian(arg_keys[0], (NLAT, NLON // BLOCK, LEV, BLOCK), 1.0, 6.0, ((0, 4), (1, 8)), jnp.float32),
        "lat_weights": jnp.clip(jax.random.uniform(arg_keys[1], (NB, 3), jnp.float32, 0.2, 1.0), 0.2, 1.0),
        "block_offsets": draw_block_offsets(jax.random.fold_in(arg_keys[6], 71), 0),
        "filters": gaussian(arg_keys[3], (NB, KB, BLOCK, BLOCK), (BLOCK * KB) ** -0.5, 0.25),
        "vertical": gaussian(arg_keys[4], (NB, LEV, LEV), LEV ** -0.5, 0.5),
        "slot_of_band": jax.random.permutation(arg_keys[5], NB).astype(jnp.int32),
    }


def reference(grad_field, lat_weights, block_offsets, filters, vertical, slot_of_band):
    padded = jnp.pad(grad_field, ((1, 1), (0, 0), (0, 0), (0, 0)))

    def one_band(items):
        weights, offsets, filter_set, vertical_b = items
        blended = (weights[0] * padded[:-2] + weights[1] * padded[1:-1] + weights[2] * padded[2:]).astype(jnp.bfloat16)
        shape_all = blended.shape
        running = jnp.zeros((shape_all[0] * shape_all[1] * shape_all[2], shape_all[3]), jnp.float32)
        for position in range(KB):
            moved = jnp.roll(blended, -offsets[position], axis=1)
            running = running + jnp.dot(moved.reshape(-1, shape_all[3]), filter_set[position], preferred_element_type=jnp.float32)
        smoothed = running.astype(jnp.bfloat16).reshape(shape_all)
        result = jnp.einsum("ml,rqlc->rqmc", vertical_b.astype(jnp.float32), smoothed.astype(jnp.float32))
        return result.astype(jnp.bfloat16)

    results = lax.map(one_band, (lat_weights, block_offsets, filters, vertical))
    return jnp.zeros_like(results).at[slot_of_band].set(results)
```

```python
import functools

import jax
import jax.numpy as jnp
from jax import lax
from jax.experimental import pallas as pl
from jax.experimental.pallas import tpu as pltpu
from jax.sharding import PartitionSpec as P

REACH = 3


def round_up(value, step):
    return (value + step - 1) // step * step


def owned_tables(lat_weights, block_offsets, filters, vertical, slot_of_band):
    band_count = slot_of_band.shape[0]
    group = band_count // lax.axis_size("lat")
    slots = lax.axis_index("lat") * group + jnp.arange(group, dtype=jnp.int32)
    bands = jnp.argmax(slot_of_band[None, :] == slots[:, None], axis=1)
    return tuple(jnp.take(t, bands, axis=0) for t in (lat_weights, block_offsets, filters, vertical))


def paired_filters(offsets, filters):
    group, _, c, d = filters.shape
    width = 2 * REACH + 1
    named = (offsets[:, None, :] + REACH == jnp.arange(width)[None, :, None])[..., None, None]
    dense = jnp.sum(jnp.where(named, filters[:, None], 0), axis=2, dtype=filters.dtype)
    left = jnp.pad(dense, ((0, 0), (0, 1), (0, 0), (0, 0)))
    right = jnp.pad(dense, ((0, 0), (1, 0), (0, 0), (0, 0)))
    both = jnp.concatenate([left, right], axis=3)
    return both.reshape(group, (width + 1) // 2, 2 * c, 2 * d)


def row_coefficients(weights, rows, row_total):
    place = lax.axis_index("lon")
    even = (place % 2 == 0).astype(jnp.float32)
    above = jnp.where(place > 0, 1.0, 0.0)
    below = jnp.where((place + 1) * rows < row_total, 1.0, 0.0)
    w0, w1, w2 = weights[:, 0], weights[:, 1], weights[:, 2]
    zero = jnp.zeros_like(w0)
    first = jnp.stack([w0 * even * above, w0 * (1 - even) * above, w1, w2], axis=1)
    second = jnp.stack([w2 * (1 - even) * below, w2 * even * below, w0, w1], axis=1)
    del zero
    return jnp.stack([first, second], axis=1)


def band_kernel(levels, coef_ref, main_ref, outer_ref, inner_ref, filt_ref, vert_ref, out_ref, window, spread):
    r, b = pl.program_id(0), pl.program_id(1)
    sources, _, per_source, padded, c = main_ref.shape
    blocks = sources * per_source
    half = blocks // 2
    taps = filt_ref.shape[1]
    k_outer, k_inner = coef_ref[b, r, 0], coef_ref[b, r, 1]
    k_first, k_second = coef_ref[b, r, 2], coef_ref[b, r, 3]

    def blend(e, _):
        parts = []
        for i in range(2):
            q = lax.rem(2 * e - REACH + i + blocks, blocks)
            s, n = q // per_source, lax.rem(q, per_source)
            value = (
                k_outer * outer_ref[s, 0, n].astype(jnp.float32)
                + k_inner * inner_ref[s, 0, n].astype(jnp.float32)
                + k_first * main_ref[s, 0, n].astype(jnp.float32)
                + k_second * main_ref[s, 1, n].astype(jnp.float32)
            )
            parts.append(value.astype(jnp.bfloat16))
        window[e] = jnp.concatenate(parts, axis=-1)
        return 0

    lax.fori_loop(0, half, blend, 0)
    for e in range(taps - 1):
        window[half + e] = window[e]

    step = 2
    vert = vert_ref[0]

    def apply(j, _):
        total = None
        for t in range(taps):
            lhs = window[pl.ds(j * step + t, step)].reshape(step * padded, 2 * c)
            term = jnp.dot(lhs, filt_ref[0, t], preferred_element_type=jnp.float32)
            total = term if total is None else total + term
        smoothed = total.astype(jnp.bfloat16)
        for i in range(step):
            mixed = jnp.dot(vert, smoothed[i * padded : (i + 1) * padded], preferred_element_type=jnp.float32)
            q = 2 * (j * step + i)
            for h in range(2):
                spread[pl.ds(q + h, padded, stride=blocks), :] = mixed[:, h * c : (h + 1) * c]
        return 0

    lax.fori_loop(0, half // step, apply, 0)
    out_ref[0, 0] = spread[: levels * blocks].reshape(levels, blocks, c).astype(jnp.bfloat16)


def band_outputs(coef, main, outer, inner, filt, vert, levels):
    sources, rows, per_source, padded, c = main.shape
    group, taps = filt.shape[:2]
    blocks = sources * per_source
    whole = lambda a: pl.BlockSpec(a.shape, lambda r, b: (0,) * a.ndim)
    flops = 2 * group * rows * blocks * padded * (taps * 2 * c * c * 2 // 2 + padded * c)
    return pl.pallas_call(
        functools.partial(band_kernel, levels),
        grid=(rows, group),
        in_specs=[
            pl.BlockSpec(memory_space=pltpu.SMEM),
            whole(main),
            whole(outer),
            whole(inner),
            pl.BlockSpec((1,) + filt.shape[1:], lambda r, b: (b, 0, 0, 0)),
            pl.BlockSpec((1,) + vert.shape[1:], lambda r, b: (b, 0, 0)),
        ],
        out_specs=pl.BlockSpec((1, 1, levels, blocks, c), lambda r, b: (b, r, 0, 0, 0)),
        out_shape=jax.ShapeDtypeStruct((group, rows, levels, blocks, c), jnp.bfloat16),
        scratch_shapes=[
            pltpu.VMEM((blocks // 2 + taps - 1, padded, 2 * c), jnp.bfloat16),
            pltpu.VMEM((padded * blocks, c), jnp.float32),
        ],
        compiler_params=pltpu.CompilerParams(vmem_limit_bytes=56 * 1024 * 1024),
        cost_estimate=pl.CostEstimate(flops=flops, bytes_accessed=10_000_000, transcendentals=0),
    )(coef, main, outer, inner, filt, vert)


def on_device(grad_field, lat_weights, block_offsets, filters, vertical, slot_of_band):
    levels = grad_field.shape[2]
    padded = round_up(levels, 16)
    sources = lax.axis_size("lon")
    weights, offsets, filters_g, vertical_g = owned_tables(
        lat_weights, block_offsets, filters, vertical, slot_of_band
    )
    filt = paired_filters(offsets, filters_g)
    extra = padded - levels
    vert = jnp.pad(vertical_g, ((0, 0), (0, extra), (0, extra)))

    own = jnp.pad(grad_field.astype(jnp.bfloat16), ((0, 0), (0, 0), (0, extra), (0, 0)))
    columns = lax.all_gather(own, "lat", axis=0, tiled=True)
    row_total = columns.shape[0]
    rows = row_total // sources
    coef = row_coefficients(weights, rows, row_total)
    by_place = columns.reshape((sources, rows) + columns.shape[1:])
    outer_rows = [max(p * rows - 1, 0) if p % 2 == 0 else min((p + 1) * rows, row_total - 1) for p in range(sources)]
    outer_send = jnp.stack([columns[i : i + 1] for i in outer_rows])
    main = lax.all_to_all(by_place, "lon", split_axis=0, concat_axis=0)
    outer = lax.all_to_all(outer_send, "lon", split_axis=0, concat_axis=0)
    even = lax.axis_index("lon") % 2 == 0
    give = jnp.where(even, main[:, 1:2], main[:, 0:1])
    inner = lax.ppermute(give, "lon", [(i, i ^ 1) for i in range(sources)])
    result = band_outputs(coef, main, outer, inner, filt, vert, levels)
    return result.transpose(0, 1, 3, 2, 4)


def solution(mesh):
    placed = (P("lat", "lon", None, None), P(), P(), P(), P(), P())
    return jax.shard_map(
        on_device,
        mesh=mesh,
        in_specs=placed,
        out_specs=P("lat", "lon", None, None, None),
        check_vma=False,
    )
```

```python
import functools

import jax
import jax.numpy as jnp
from jax import lax
from jax.experimental import pallas as pl
from jax.experimental.pallas import tpu as pltpu
from jax.sharding import PartitionSpec as P

REACH = 3
SUBLANES = 16
SPREAD_GAP = 8
CUTS = (48, 96)


SCALAR = pl.BlockSpec(memory_space=pltpu.SMEM)
PARAMS = pltpu.CompilerParams(vmem_limit_bytes=20 * 1024 * 1024)


def round_up(value, step):
    return (value + step - 1) // step * step


def band_of(slot_ref, slot):
    band = 0
    for i in range(slot_ref.shape[0]):
        band = jnp.where(slot_ref[i] == slot, i, band)
    return band


def table_kernel(where_ref, slot_ref, offset_ref, filter_ref, vertical_ref, filt_out, vert_out):
    group, _, c, _ = filt_out.shape
    levels = vertical_ref.shape[1]
    filt_out[...] = jnp.zeros_like(filt_out)
    vert_out[...] = jnp.zeros_like(vert_out)
    for g in range(group):
        band = band_of(slot_ref, where_ref[1] * group + g)
        for k in range(filter_ref.shape[1]):
            n = offset_ref[band, k] + REACH
            for h in range(2):
                filt_out[g, n + h, :, h * c : (h + 1) * c] = filter_ref[band, k]
        vert_out[g, :levels, :levels] = vertical_ref[band]


def owned_tables(where, slot_of_band, block_offsets, filters, vertical, group, padded):
    c = filters.shape[-1]
    vmem = pl.BlockSpec(memory_space=pltpu.VMEM)
    filt, vert = pl.pallas_call(
        table_kernel,
        in_specs=[SCALAR] * 3 + [vmem] * 2,
        out_specs=[vmem] * 2,
        out_shape=[
            jax.ShapeDtypeStruct((group, 2 * REACH + 2, c, 2 * c), filters.dtype),
            jax.ShapeDtypeStruct((group, padded, padded), vertical.dtype),
        ],
        compiler_params=PARAMS,
        cost_estimate=pl.CostEstimate(flops=0, bytes_accessed=4_000_000, transcendentals=0),
    )(where, slot_of_band, block_offsets, filters, vertical)
    return filt.reshape(group, REACH + 1, 2 * c, 2 * c), vert


def row_weights(where_ref, slot_ref, weight_ref, r, b, rows, row_total):
    group = slot_ref.shape[0] // where_ref[3]
    band = band_of(slot_ref, where_ref[1] * group + b)
    row = where_ref[0] * rows + r
    above = jnp.where(row > 0, weight_ref[band, 0], 0.0)
    below = jnp.where(row + 1 < row_total, weight_ref[band, 2], 0.0)
    return above, weight_ref[band, 1], below


def fill_window(window, place, weights, r, sides):
    chips = len(sides[0])
    shard_rows, per_source, _, c = sides[0][0].shape
    half = chips * per_source
    first = lax.rem(place, 2) * ((shard_rows - 2) // 2) + r
    for k in range(chips):
        for side in range(2):
            source = (place ^ (2 * k)) ^ side
            for n in range(per_source):
                value = None
                for i in range(3):
                    term = weights[i] * sides[side][k][first + i, n].astype(jnp.float32)
                    value = term if value is None else value + term
                e = lax.rem(source * (per_source // 2) + (n + REACH) // 2, half)
                lane = (n + REACH) % 2 * c
                window[e, :, lane : lane + c] = value.astype(jnp.bfloat16)
    for e in range(window.shape[0] - half):
        window[half + e] = window[e]


def filtered(window, filt, j, step):
    _, depth, width = window.shape
    total = None
    for t in range(filt.shape[0]):
        lhs = window[j + t : j + t + step].reshape(step * depth, width)
        term = jnp.dot(lhs, filt[t], preferred_element_type=jnp.float32)
        total = term if total is None else total + term
    return total.astype(jnp.bfloat16)


def first_kernel(chips, where_ref, slot_ref, weight_ref, *refs):
    kept, got, (filt_ref, out_ref, window) = refs[:chips], refs[chips : 2 * chips], refs[2 * chips :]
    r, b = pl.program_id(0), pl.program_id(1)
    rows = (kept[0].shape[0] - 2) // 2
    weights = row_weights(where_ref, slot_ref, weight_ref, r, b, rows, 2 * rows * chips)
    fill_window(window, where_ref[0], weights, r, (kept, got))
    half, depth, width = out_ref.shape[2:]
    step = 4
    for j in range(0, half, step):
        out_ref[0, 0, j : j + step] = filtered(window, filt_ref[0], j, step).reshape(step, depth, width)


def last_kernel(chips, where_ref, slot_ref, weight_ref, *refs):
    kept, got, refs = refs[:chips], refs[chips : 2 * chips], refs[2 * chips :]
    filt_ref, vert_ref = refs[:2]
    done, (out_ref, window, spread) = refs[2:-3], refs[-3:]
    r, b = pl.program_id(0), pl.program_id(1)
    rows = (kept[0].shape[0] - 2) // 2
    weights = row_weights(where_ref, slot_ref, weight_ref, r, b, rows, 2 * rows * chips)
    fill_window(window, where_ref[0], weights, r, (kept, got))
    levels, blocks, c = out_ref.shape[2:]
    half, depth = blocks // 2, window.shape[1]
    padded = vert_ref.shape[1]
    pitch = spread.shape[0] // padded
    step = 4
    for j in range(0, half, step):
        later = filtered(window, filt_ref[0], j, step)
        for i in range(step):
            column = [d[0, 0, j + i] for d in done] + [later[i * depth : (i + 1) * depth]]
            column = jnp.concatenate(column, axis=0)
            mixed = jnp.dot(vert_ref[0], column, preferred_element_type=jnp.float32)
            for h in range(2):
                spread[pl.ds(2 * (j + i) + h, padded, stride=pitch), :] = mixed[:, h * c : (h + 1) * c]
    for m in range(levels):
        out_ref[0, 0, m] = spread[m * pitch : m * pitch + blocks].astype(jnp.bfloat16)


def whole(a):
    return pl.BlockSpec(a.shape, lambda r, b: (0,) * a.ndim)


def banded(a):
    return pl.BlockSpec((1,) + a.shape[1:], lambda r, b: (b,) + (0,) * (a.ndim - 1))


def by_row_and_band(a):
    return pl.BlockSpec((1, 1) + a.shape[2:], lambda r, b: (b, r) + (0,) * (a.ndim - 2))


def first_part(scalars, kept, got, filt, rows):
    group, taps, width, _ = filt.shape
    _, per_source, depth, _ = kept[0].shape
    half = len(kept) * per_source
    out = jax.ShapeDtypeStruct((group, rows, half, depth, width), jnp.bfloat16)
    return pl.pallas_call(
        functools.partial(first_kernel, len(kept)),
        grid=(rows, group),
        in_specs=[SCALAR] * 3 + [whole(m) for m in kept + got] + [banded(filt)],
        out_specs=by_row_and_band(out),
        out_shape=out,
        scratch_shapes=[pltpu.VMEM((half + taps - 1, depth, width), jnp.bfloat16)],
        compiler_params=PARAMS,
        cost_estimate=pl.CostEstimate(flops=2_000_000_000, bytes_accessed=8_000_000, transcendentals=0),
    )(*scalars, *kept, *got, filt)


def last_part(scalars, kept, got, filt, vert, done, rows, levels):
    group, taps, width, _ = filt.shape
    _, per_source, depth, c = kept[0].shape
    half = len(kept) * per_source
    padded = vert.shape[1]
    out = jax.ShapeDtypeStruct((group, rows, levels, 2 * half, c), jnp.bfloat16)
    return pl.pallas_call(
        functools.partial(last_kernel, len(kept)),
        grid=(rows, group),
        in_specs=[SCALAR] * 3
        + [whole(m) for m in kept + got]
        + [banded(filt), banded(vert)]
        + [by_row_and_band(d) for d in done],
        out_specs=by_row_and_band(out),
        out_shape=out,
        scratch_shapes=[
            pltpu.VMEM((half + taps - 1, depth, width), jnp.bfloat16),
            pltpu.VMEM((padded * (2 * half + SPREAD_GAP), c), jnp.float32),
        ],
        compiler_params=PARAMS,
        cost_estimate=pl.CostEstimate(flops=4_000_000_000, bytes_accessed=12_000_000, transcendentals=0),
    )(*scalars, *kept, *got, filt, vert, *done)


def swapped(value, axis, by):
    return lax.ppermute(value, axis, [(i, i ^ by) for i in range(lax.axis_size(axis))])


def sort_kernel(where_ref, *refs):
    count = (len(refs) - 1) // 2
    pieces, outs, sems = refs[:count], refs[count:-1], refs[-1]
    shard_rows = pieces[0].shape[0]
    chip, z = where_ref[0] // 2, where_ref[1]

    def copies(k, piece):
        main = pltpu.make_async_copy(piece, outs[k].at[pl.ds(1, shard_rows)], sems.at[k, 0])
        above = pltpu.make_async_copy(piece.at[pl.ds(shard_rows - 1, 1)], outs[k].at[pl.ds(0, 1)], sems.at[k, 1])
        below = pltpu.make_async_copy(piece.at[pl.ds(0, 1)], outs[k].at[pl.ds(shard_rows + 1, 1)], sems.at[k, 2])
        return main, above, below

    for k in range(count):
        plane = chip ^ k
        for j, piece in enumerate(pieces):
            main, above, below = copies(k, piece)
            pl.when((plane ^ z) == j)(main.start)
            pl.when((jnp.maximum(plane - 1, 0) ^ z) == j)(above.start)
            pl.when((jnp.minimum(plane + 1, count - 1) ^ z) == j)(below.start)
    for k in range(count):
        for copy in copies(k, pieces[0]):
            copy.wait()


def sorted_rows(where, pieces):
    shape = pieces[0].shape
    out = jax.ShapeDtypeStruct((shape[0] + 2,) + shape[1:], pieces[0].dtype)
    anywhere = pl.BlockSpec(memory_space=pl.ANY)
    return pl.pallas_call(
        sort_kernel,
        in_specs=[SCALAR] + [anywhere] * len(pieces),
        out_specs=[anywhere] * len(pieces),
        out_shape=[out] * len(pieces),
        scratch_shapes=[pltpu.SemaphoreType.DMA((len(pieces), 3))],
        compiler_params=PARAMS,
        cost_estimate=pl.CostEstimate(flops=0, bytes_accessed=3_000_000, transcendentals=0),
    )(where, *pieces)


def along_lat(own):
    order = sorted(range(1, lax.axis_size("lat")), key=lambda j: j == 1)
    got = {j: swapped(own, "lat", j) for j in order}
    return [own] + [got[j] for j in sorted(got)]


def along_lon(sends):
    order = sorted(range(1, len(sends)), key=lambda k: -k)
    got = {k: swapped(sends[k], "lon", 2 * k) for k in order}
    kept = [sends[0]] + [got[k] for k in sorted(got)]
    return kept, [swapped(m, "lon", 1) for m in kept]


def on_device(grad_field, lat_weights, block_offsets, filters, vertical, slot_of_band):
    shard_rows, _, levels, _ = grad_field.shape
    lats, lons = lax.axis_size("lat"), lax.axis_size("lon")
    rows = shard_rows * lats // lons
    group = slot_of_band.shape[0] // lats
    padded = round_up(levels, SUBLANES)
    extra = padded - levels
    cuts = [0] + list(CUTS) + [padded]

    place = [lax.axis_index("lon"), lax.axis_index("lat"), jnp.int32(lons), jnp.int32(lats)]
    where = jnp.stack(place).astype(jnp.int32)
    scalars = (where, slot_of_band, lat_weights)
    filt, vert = owned_tables(where, slot_of_band, block_offsets, filters, vertical, group, padded)

    own = jnp.pad(grad_field.astype(jnp.bfloat16), ((0, 0), (0, 0), (0, extra), (0, 0)))
    parts = [own[:, :, lo:hi] for lo, hi in zip(cuts, cuts[1:])]
    pieces = []
    for part in parts:
        if pieces:
            part, _ = lax.optimization_barrier((part, pieces[-1][2]))
        pieces.append(along_lat(part))
    sides = [along_lon(sorted_rows(where, piece)) for piece in pieces]
    done = [first_part(scalars, kept, got, filt, rows) for kept, got in sides[:-1]]
    kept, got = sides[-1]
    result = last_part(scalars, kept, got, filt, vert, done, rows, levels)
    return result.transpose(0, 1, 3, 2, 4)


def solution(mesh):
    placed = (P("lat", "lon", None, None), P(), P(), P(), P(), P())
    return jax.shard_map(
        on_device,
        mesh=mesh,
        in_specs=placed,
        out_specs=P("lat", "lon", None, None, None),
        check_vma=False,
    )
```

```python
import functools

import jax
import jax.numpy as jnp
from jax import lax
from jax.experimental import pallas as pl
from jax.experimental.pallas import tpu as pltpu
from jax.sharding import PartitionSpec as P

REACH = 3
SUBLANES = 16
SPREAD_GAP = 8
CUTS = (48, 112)


SCALAR = pl.BlockSpec(memory_space=pltpu.SMEM)
PARAMS = pltpu.CompilerParams(vmem_limit_bytes=20 * 1024 * 1024)


def round_up(value, step):
    return (value + step - 1) // step * step


def band_of(slot_ref, slot):
    band = 0
    for i in range(slot_ref.shape[0]):
        band = jnp.where(slot_ref[i] == slot, i, band)
    return band


def table_kernel(where_ref, slot_ref, offset_ref, filter_ref, vertical_ref, filt_out, vert_out):
    group, _, c, _ = filt_out.shape
    levels = vertical_ref.shape[1]
    filt_out[...] = jnp.zeros_like(filt_out)
    vert_out[...] = jnp.zeros_like(vert_out)
    for g in range(group):
        band = band_of(slot_ref, where_ref[1] * group + g)
        for k in range(filter_ref.shape[1]):
            n = offset_ref[band, k] + REACH
            for h in range(2):
                filt_out[g, n + h, :, h * c : (h + 1) * c] = filter_ref[band, k]
        vert_out[g, :levels, :levels] = vertical_ref[band]


def owned_tables(where, slot_of_band, block_offsets, filters, vertical, group, padded):
    c = filters.shape[-1]
    vmem = pl.BlockSpec(memory_space=pltpu.VMEM)
    filt, vert = pl.pallas_call(
        table_kernel,
        in_specs=[SCALAR] * 3 + [vmem] * 2,
        out_specs=[vmem] * 2,
        out_shape=[
            jax.ShapeDtypeStruct((group, 2 * REACH + 2, c, 2 * c), filters.dtype),
            jax.ShapeDtypeStruct((group, padded, padded), vertical.dtype),
        ],
        compiler_params=PARAMS,
        cost_estimate=pl.CostEstimate(flops=0, bytes_accessed=4_000_000, transcendentals=0),
    )(where, slot_of_band, block_offsets, filters, vertical)
    return filt.reshape(group, REACH + 1, 2 * c, 2 * c), vert


def row_weights(where_ref, slot_ref, weight_ref, r, b, rows, row_total):
    group = slot_ref.shape[0] // where_ref[3]
    band = band_of(slot_ref, where_ref[1] * group + b)
    row = where_ref[0] * rows + r
    above = jnp.where(row > 0, weight_ref[band, 0], 0.0)
    below = jnp.where(row + 1 < row_total, weight_ref[band, 2], 0.0)
    return above, weight_ref[band, 1], below


def fill_window(window, place, weights, r, kept, got):
    chips = len(kept)
    shard_rows, per_source, _, c = kept[0].shape
    half = chips * per_source
    first = lax.rem(place, 2) * ((shard_rows - 2) // 2) + r
    for k in range(chips):
        for side in range(2):
            source = (place ^ (2 * k)) ^ side
            for n in range(per_source):
                value = None
                for i in range(3):
                    if side == 0:
                        row = kept[k][first + i, n]
                    elif len(got[0].shape) == 5:
                        row = got[0][k, r + i, n]
                    else:
                        row = got[k][first + i, n]
                    term = weights[i] * row.astype(jnp.float32)
                    value = term if value is None else value + term
                e = lax.rem(source * (per_source // 2) + (n + REACH) // 2, half)
                lane = (n + REACH) % 2 * c
                window[e, :, lane : lane + c] = value.astype(jnp.bfloat16)
    for e in range(window.shape[0] - half):
        window[half + e] = window[e]


def filtered(window, filt, j, step):
    _, depth, width = window.shape
    total = None
    for t in range(filt.shape[0]):
        lhs = window[j + t : j + t + step].reshape(step * depth, width)
        term = jnp.dot(lhs, filt[t], preferred_element_type=jnp.float32)
        total = term if total is None else total + term
    return total.astype(jnp.bfloat16)


def first_kernel(chips, where_ref, slot_ref, weight_ref, *refs):
    kept, got, (filt_ref, out_ref, window) = refs[:chips], refs[chips:-3], refs[-3:]
    r, b = pl.program_id(0), pl.program_id(1)
    rows = (kept[0].shape[0] - 2) // 2
    weights = row_weights(where_ref, slot_ref, weight_ref, r, b, rows, 2 * rows * chips)
    fill_window(window, where_ref[0], weights, r, kept, got)
    half, depth, width = out_ref.shape[2:]
    step = 4
    for j in range(0, half, step):
        out_ref[0, 0, j : j + step] = filtered(window, filt_ref[0], j, step).reshape(step, depth, width)


def last_kernel(chips, where_ref, slot_ref, weight_ref, *refs):
    kept, got, refs = refs[:chips], refs[chips : 2 * chips], refs[2 * chips :]
    filt_ref, vert_ref = refs[:2]
    done, (out_ref, window, spread) = refs[2:-3], refs[-3:]
    r, b = pl.program_id(0), pl.program_id(1)
    rows = (kept[0].shape[0] - 2) // 2
    weights = row_weights(where_ref, slot_ref, weight_ref, r, b, rows, 2 * rows * chips)
    fill_window(window, where_ref[0], weights, r, kept, got)
    levels, blocks, c = out_ref.shape[2:]
    half, depth = blocks // 2, window.shape[1]
    padded = vert_ref.shape[1]
    pitch = spread.shape[0] // padded
    step = 4
    for j in range(0, half, step):
        later = filtered(window, filt_ref[0], j, step)
        for i in range(step):
            column = [d[0, 0, j + i] for d in done] + [later[i * depth : (i + 1) * depth]]
            column = jnp.concatenate(column, axis=0)
            mixed = jnp.dot(vert_ref[0], column, preferred_element_type=jnp.float32)
            for h in range(2):
                spread[pl.ds(2 * (j + i) + h, padded, stride=pitch), :] = mixed[:, h * c : (h + 1) * c]
    for m in range(levels):
        out_ref[0, 0, m] = spread[m * pitch : m * pitch + blocks].astype(jnp.bfloat16)


def whole(a):
    return pl.BlockSpec(a.shape, lambda r, b: (0,) * a.ndim)


def banded(a):
    return pl.BlockSpec((1,) + a.shape[1:], lambda r, b: (b,) + (0,) * (a.ndim - 1))


def by_row_and_band(a):
    return pl.BlockSpec((1, 1) + a.shape[2:], lambda r, b: (b, r) + (0,) * (a.ndim - 2))


def first_part(scalars, kept, got, filt, rows):
    group, taps, width, _ = filt.shape
    _, per_source, depth, _ = kept[0].shape
    half = len(kept) * per_source
    out = jax.ShapeDtypeStruct((group, rows, half, depth, width), jnp.bfloat16)
    return pl.pallas_call(
        functools.partial(first_kernel, len(kept)),
        grid=(rows, group),
        in_specs=[SCALAR] * 3 + [whole(m) for m in kept + got] + [banded(filt)],
        out_specs=by_row_and_band(out),
        out_shape=out,
        scratch_shapes=[pltpu.VMEM((half + taps - 1, depth, width), jnp.bfloat16)],
        compiler_params=PARAMS,
        cost_estimate=pl.CostEstimate(flops=2_000_000_000, bytes_accessed=8_000_000, transcendentals=0),
    )(*scalars, *kept, *got, filt)


def last_part(scalars, kept, got, filt, vert, done, rows, levels):
    group, taps, width, _ = filt.shape
    _, per_source, depth, c = kept[0].shape
    half = len(kept) * per_source
    padded = vert.shape[1]
    out = jax.ShapeDtypeStruct((group, rows, levels, 2 * half, c), jnp.bfloat16)
    return pl.pallas_call(
        functools.partial(last_kernel, len(kept)),
        grid=(rows, group),
        in_specs=[SCALAR] * 3
        + [whole(m) for m in kept + got]
        + [banded(filt), banded(vert)]
        + [by_row_and_band(d) for d in done],
        out_specs=by_row_and_band(out),
        out_shape=out,
        scratch_shapes=[
            pltpu.VMEM((half + taps - 1, depth, width), jnp.bfloat16),
            pltpu.VMEM((padded * (2 * half + SPREAD_GAP), c), jnp.float32),
        ],
        compiler_params=PARAMS,
        cost_estimate=pl.CostEstimate(flops=4_000_000_000, bytes_accessed=12_000_000, transcendentals=0),
    )(*scalars, *kept, *got, filt, vert, *done)


def swapped(value, axis, by):
    return lax.ppermute(value, axis, [(i, i ^ by) for i in range(lax.axis_size(axis))])


def sort_kernel(where_ref, *refs):
    count = (len(refs) - 1) // 2
    pieces, outs, sems = refs[:count], refs[count:-1], refs[-1]
    shard_rows = pieces[0].shape[0]
    chip, z = where_ref[0] // 2, where_ref[1]

    def copies(k, piece):
        main = pltpu.make_async_copy(piece, outs[k].at[pl.ds(1, shard_rows)], sems.at[k, 0])
        above = pltpu.make_async_copy(piece.at[pl.ds(shard_rows - 1, 1)], outs[k].at[pl.ds(0, 1)], sems.at[k, 1])
        below = pltpu.make_async_copy(piece.at[pl.ds(0, 1)], outs[k].at[pl.ds(shard_rows + 1, 1)], sems.at[k, 2])
        return main, above, below

    for k in range(count):
        plane = chip ^ k
        for j, piece in enumerate(pieces):
            main, above, below = copies(k, piece)
            pl.when((plane ^ z) == j)(main.start)
            pl.when((jnp.maximum(plane - 1, 0) ^ z) == j)(above.start)
            pl.when((jnp.minimum(plane + 1, count - 1) ^ z) == j)(below.start)
    for k in range(count):
        for copy in copies(k, pieces[0]):
            copy.wait()


def sorted_rows(where, pieces):
    shape = pieces[0].shape
    out = jax.ShapeDtypeStruct((shape[0] + 2,) + shape[1:], pieces[0].dtype)
    anywhere = pl.BlockSpec(memory_space=pl.ANY)
    return pl.pallas_call(
        sort_kernel,
        in_specs=[SCALAR] + [anywhere] * len(pieces),
        out_specs=[anywhere] * len(pieces),
        out_shape=[out] * len(pieces),
        scratch_shapes=[pltpu.SemaphoreType.DMA((len(pieces), 3))],
        compiler_params=PARAMS,
        cost_estimate=pl.CostEstimate(flops=0, bytes_accessed=3_000_000, transcendentals=0),
    )(where, *pieces)


def along_lat(own):
    pieces = {0: own}
    step = lax.axis_size("lat") // 2
    while step:
        pieces.update({j | step: swapped(piece, "lat", step) for j, piece in list(pieces.items())})
        step //= 2
    return [pieces[j] for j in range(len(pieces))]


def along_lon(sends):
    order = sorted(range(1, len(sends)), key=lambda k: -k)
    got = {k: swapped(sends[k], "lon", 2 * k) for k in order}
    return [sends[0]] + [got[k] for k in sorted(got)]


def after(value, *marks):
    return lax.optimization_barrier((value, marks))[0]


def on_device(grad_field, lat_weights, block_offsets, filters, vertical, slot_of_band):
    shard_rows, _, levels, _ = grad_field.shape
    lats, lons = lax.axis_size("lat"), lax.axis_size("lon")
    rows = shard_rows * lats // lons
    group = slot_of_band.shape[0] // lats
    padded = round_up(levels, SUBLANES)
    extra = padded - levels
    cuts = [0] + list(CUTS) + [padded]

    place = [lax.axis_index("lon"), lax.axis_index("lat"), jnp.int32(lons), jnp.int32(lats)]
    where = jnp.stack(place).astype(jnp.int32)
    scalars = (where, slot_of_band, lat_weights)
    filt, vert = owned_tables(where, slot_of_band, block_offsets, filters, vertical, group, padded)

    own = jnp.pad(grad_field.astype(jnp.bfloat16), ((0, 0), (0, 0), (0, extra), (0, 0)))
    parts = [own[:, :, lo:hi] for lo, hi in zip(cuts, cuts[1:])]
    last = len(parts) - 1
    pieces = []
    for part in parts:
        pieces.append(along_lat(after(part, pieces[-1][2]) if pieces else part))
    sends = [sorted_rows(where, piece) for piece in pieces]
    kept = [along_lon(send) for send in sends]
    done = []
    for i in range(last):
        here = after(kept[i], sends[i + 1])
        got = [swapped(m, "lon", 1) for m in here]
        done.append(first_part(scalars, here, got, filt, rows))
    here = kept[last][:1] + after(kept[last][1:], *done)
    got = [swapped(m, "lon", 1) for m in here]
    result = last_part(scalars, here, got, filt, vert, done, rows, levels)
    return result.transpose(0, 1, 3, 2, 4)


def solution(mesh):
    placed = (P("lat", "lon", None, None), P(), P(), P(), P(), P())
    return jax.shard_map(
        on_device,
        mesh=mesh,
        in_specs=placed,
        out_specs=P("lat", "lon", None, None, None),
        check_vma=False,
    )
```

```python
import functools

import jax
import jax.numpy as jnp
from jax import lax
from jax.experimental import pallas as pl
from jax.experimental.pallas import tpu as pltpu
from jax.sharding import PartitionSpec as P

REACH = 3
SUBLANES = 16
LANES = 128
SPREAD_GAP = 8
CUTS = (48, 112)


SCALAR = pl.BlockSpec(memory_space=pltpu.SMEM)
PARAMS = pltpu.CompilerParams(vmem_limit_bytes=20 * 1024 * 1024)


def round_up(value, step):
    return (value + step - 1) // step * step


def band_of(slot_ref, slot):
    band = 0
    for i in range(slot_ref.shape[0]):
        band = jnp.where(slot_ref[i] == slot, i, band)
    return band


def table_kernel(where_ref, slot_ref, offset_ref, filter_ref, vertical_ref, filt_out, vert_out, lines):
    group, _, c, _ = filt_out.shape
    levels, bands, _ = vertical_ref.shape
    strips = [(lo, min(LANES, levels - lo)) for lo in range(0, levels, LANES)]
    for i, (lo, size) in enumerate(strips):
        strip = vertical_ref[:, :, lo : lo + size].astype(jnp.float32)
        lines[i, :, :size] = strip.reshape(levels * bands, size)
    filt_out[...] = jnp.zeros_like(filt_out)
    vert_out[...] = jnp.zeros_like(vert_out)
    for g in range(group):
        band = band_of(slot_ref, where_ref[1] * group + g)
        for k in range(filter_ref.shape[1]):
            n = offset_ref[band, k] + REACH
            for h in range(2):
                filt_out[g, n + h, :, h * c : (h + 1) * c] = filter_ref[band, k]
        for i, (lo, size) in enumerate(strips):
            strip = lines[i, pl.ds(band, levels, stride=bands), :]
            vert_out[g, :levels, lo : lo + size] = strip[:, :size].astype(vert_out.dtype)


def owned_tables(where, slot_of_band, block_offsets, filters, vertical, group, padded):
    c, levels = filters.shape[-1], vertical.shape[-1]
    vmem = pl.BlockSpec(memory_space=pltpu.VMEM)
    filt, vert = pl.pallas_call(
        table_kernel,
        in_specs=[SCALAR] * 3 + [vmem] * 2,
        out_specs=[vmem] * 2,
        out_shape=[
            jax.ShapeDtypeStruct((group, 2 * REACH + 2, c, 2 * c), filters.dtype),
            jax.ShapeDtypeStruct((group, padded, padded), vertical.dtype),
        ],
        scratch_shapes=[pltpu.VMEM((pl.cdiv(levels, LANES), vertical.shape[0] * levels, LANES), jnp.float32)],
        compiler_params=PARAMS,
        cost_estimate=pl.CostEstimate(flops=0, bytes_accessed=4_000_000, transcendentals=0),
    )(where, slot_of_band, block_offsets, filters, vertical.transpose(1, 0, 2))
    return filt.reshape(group, REACH + 1, 2 * c, 2 * c), vert


def row_weights(where_ref, slot_ref, weight_ref, r, b, rows, row_total):
    group = slot_ref.shape[0] // where_ref[3]
    band = band_of(slot_ref, where_ref[1] * group + b)
    row = where_ref[0] * rows + r
    above = jnp.where(row > 0, weight_ref[0, band], 0.0)
    below = jnp.where(row + 1 < row_total, weight_ref[2, band], 0.0)
    return above, weight_ref[1, band], below


def fill_window(window, place, weights, r, kept, got):
    chips = len(kept)
    shard_rows, per_source, _, c = kept[0].shape
    half = chips * per_source
    first = lax.rem(place, 2) * ((shard_rows - 2) // 2) + r
    for k in range(chips):
        for side in range(2):
            source = (place ^ (2 * k)) ^ side
            for n in range(per_source):
                value = None
                for i in range(3):
                    if side == 0:
                        row = kept[k][first + i, n]
                    elif len(got[0].shape) == 5:
                        row = got[0][k, r + i, n]
                    else:
                        row = got[k][first + i, n]
                    term = weights[i] * row.astype(jnp.float32)
                    value = term if value is None else value + term
                e = lax.rem(source * (per_source // 2) + (n + REACH) // 2, half)
                lane = (n + REACH) % 2 * c
                window[e, :, lane : lane + c] = value.astype(jnp.bfloat16)
    for e in range(window.shape[0] - half):
        window[half + e] = window[e]


def filtered(window, filt, j, step):
    _, depth, width = window.shape
    total = None
    for t in range(filt.shape[0]):
        lhs = window[j + t : j + t + step].reshape(step * depth, width)
        term = jnp.dot(lhs, filt[t], preferred_element_type=jnp.float32)
        total = term if total is None else total + term
    return total.astype(jnp.bfloat16)


def first_kernel(chips, where_ref, slot_ref, weight_ref, *refs):
    kept, got, (filt_ref, out_ref, window) = refs[:chips], refs[chips:-3], refs[-3:]
    r, b = pl.program_id(0), pl.program_id(1)
    rows = (kept[0].shape[0] - 2) // 2
    weights = row_weights(where_ref, slot_ref, weight_ref, r, b, rows, 2 * rows * chips)
    fill_window(window, where_ref[0], weights, r, kept, got)
    half, depth, width = out_ref.shape[2:]
    step = 4
    for j in range(0, half, step):
        out_ref[0, 0, j : j + step] = filtered(window, filt_ref[0], j, step).reshape(step, depth, width)


def last_kernel(chips, where_ref, slot_ref, weight_ref, *refs):
    kept, got, refs = refs[:chips], refs[chips : 2 * chips], refs[2 * chips :]
    filt_ref, vert_ref = refs[:2]
    done, (out_ref, window, spread) = refs[2:-3], refs[-3:]
    r, b = pl.program_id(0), pl.program_id(1)
    rows = (kept[0].shape[0] - 2) // 2
    weights = row_weights(where_ref, slot_ref, weight_ref, r, b, rows, 2 * rows * chips)
    fill_window(window, where_ref[0], weights, r, kept, got)
    levels, blocks, c = out_ref.shape[2:]
    half, depth = blocks // 2, window.shape[1]
    padded = vert_ref.shape[1]
    pitch = spread.shape[0] // padded
    step = 4
    for j in range(0, half, step):
        later = filtered(window, filt_ref[0], j, step)
        for i in range(step):
            column = [d[0, 0, j + i] for d in done] + [later[i * depth : (i + 1) * depth]]
            column = jnp.concatenate(column, axis=0)
            mixed = jnp.dot(vert_ref[0], column, preferred_element_type=jnp.float32)
            for h in range(2):
                spread[pl.ds(2 * (j + i) + h, padded, stride=pitch), :] = mixed[:, h * c : (h + 1) * c]
    for m in range(levels):
        out_ref[0, 0, m] = spread[m * pitch : m * pitch + blocks].astype(jnp.bfloat16)


def whole(a):
    return pl.BlockSpec(a.shape, lambda r, b: (0,) * a.ndim)


def banded(a):
    return pl.BlockSpec((1,) + a.shape[1:], lambda r, b: (b,) + (0,) * (a.ndim - 1))


def by_row_and_band(a):
    return pl.BlockSpec((1, 1) + a.shape[2:], lambda r, b: (b, r) + (0,) * (a.ndim - 2))


def first_part(scalars, kept, got, filt, rows):
    group, taps, width, _ = filt.shape
    _, per_source, depth, _ = kept[0].shape
    half = len(kept) * per_source
    out = jax.ShapeDtypeStruct((group, rows, half, depth, width), jnp.bfloat16)
    return pl.pallas_call(
        functools.partial(first_kernel, len(kept)),
        grid=(rows, group),
        in_specs=[SCALAR] * 3 + [whole(m) for m in kept + got] + [banded(filt)],
        out_specs=by_row_and_band(out),
        out_shape=out,
        scratch_shapes=[pltpu.VMEM((half + taps - 1, depth, width), jnp.bfloat16)],
        compiler_params=PARAMS,
        cost_estimate=pl.CostEstimate(flops=2_000_000_000, bytes_accessed=8_000_000, transcendentals=0),
    )(*scalars, *kept, *got, filt)


def last_part(scalars, kept, got, filt, vert, done, rows, levels):
    group, taps, width, _ = filt.shape
    _, per_source, depth, c = kept[0].shape
    half = len(kept) * per_source
    padded = vert.shape[1]
    out = jax.ShapeDtypeStruct((group, rows, levels, 2 * half, c), jnp.bfloat16)
    return pl.pallas_call(
        functools.partial(last_kernel, len(kept)),
        grid=(rows, group),
        in_specs=[SCALAR] * 3
        + [whole(m) for m in kept + got]
        + [banded(filt), banded(vert)]
        + [by_row_and_band(d) for d in done],
        out_specs=by_row_and_band(out),
        out_shape=out,
        scratch_shapes=[
            pltpu.VMEM((half + taps - 1, depth, width), jnp.bfloat16),
            pltpu.VMEM((padded * (2 * half + SPREAD_GAP), c), jnp.float32),
        ],
        compiler_params=PARAMS,
        cost_estimate=pl.CostEstimate(flops=4_000_000_000, bytes_accessed=12_000_000, transcendentals=0),
    )(*scalars, *kept, *got, filt, vert, *done)


def swapped(value, axis, by):
    return lax.ppermute(value, axis, [(i, i ^ by) for i in range(lax.axis_size(axis))])


def sort_kernel(where_ref, *refs):
    count = (len(refs) - 1) // 2
    pieces, outs, sems = refs[:count], refs[count:-1], refs[-1]
    shard_rows = pieces[0].shape[0]
    chip, z = where_ref[0] // 2, where_ref[1]

    def copies(k, piece):
        main = pltpu.make_async_copy(piece, outs[k].at[pl.ds(1, shard_rows)], sems.at[k, 0])
        above = pltpu.make_async_copy(piece.at[pl.ds(shard_rows - 1, 1)], outs[k].at[pl.ds(0, 1)], sems.at[k, 1])
        below = pltpu.make_async_copy(piece.at[pl.ds(0, 1)], outs[k].at[pl.ds(shard_rows + 1, 1)], sems.at[k, 2])
        return main, above, below

    for k in range(count):
        plane = chip ^ k
        for j, piece in enumerate(pieces):
            main, above, below = copies(k, piece)
            pl.when((plane ^ z) == j)(main.start)
            pl.when((jnp.maximum(plane - 1, 0) ^ z) == j)(above.start)
            pl.when((jnp.minimum(plane + 1, count - 1) ^ z) == j)(below.start)
    for k in range(count):
        for copy in copies(k, pieces[0]):
            copy.wait()


def sorted_rows(where, pieces):
    shape = pieces[0].shape
    out = jax.ShapeDtypeStruct((shape[0] + 2,) + shape[1:], pieces[0].dtype)
    anywhere = pl.BlockSpec(memory_space=pl.ANY)
    return pl.pallas_call(
        sort_kernel,
        in_specs=[SCALAR] + [anywhere] * len(pieces),
        out_specs=[anywhere] * len(pieces),
        out_shape=[out] * len(pieces),
        scratch_shapes=[pltpu.SemaphoreType.DMA((len(pieces), 3))],
        compiler_params=PARAMS,
        cost_estimate=pl.CostEstimate(flops=0, bytes_accessed=3_000_000, transcendentals=0),
    )(where, *pieces)


def along_lat(own):
    pieces = {0: own}
    step = lax.axis_size("lat") // 2
    while step:
        pieces.update({j | step: swapped(piece, "lat", step) for j, piece in list(pieces.items())})
        step //= 2
    return [pieces[j] for j in range(len(pieces))]


def along_lon(sends):
    order = sorted(range(1, len(sends)), key=lambda k: -k)
    got = {k: swapped(sends[k], "lon", 2 * k) for k in order}
    return [sends[0]] + [got[k] for k in sorted(got)]


def after(value, *marks):
    return lax.optimization_barrier((value, marks))[0]


def on_device(grad_field, lat_weights, block_offsets, filters, vertical, slot_of_band):
    shard_rows, _, levels, _ = grad_field.shape
    lats, lons = lax.axis_size("lat"), lax.axis_size("lon")
    rows = shard_rows * lats // lons
    group = slot_of_band.shape[0] // lats
    padded = round_up(levels, SUBLANES)
    extra = padded - levels
    cuts = [0] + list(CUTS) + [padded]

    place = [lax.axis_index("lon"), lax.axis_index("lat"), jnp.int32(lons), jnp.int32(lats)]
    where = jnp.stack(place).astype(jnp.int32)
    scalars = (where, slot_of_band, lat_weights.T)
    filt, vert = owned_tables(where, slot_of_band, block_offsets, filters, vertical, group, padded)

    own = jnp.pad(grad_field.astype(jnp.bfloat16), ((0, 0), (0, 0), (0, extra), (0, 0)))
    parts = [own[:, :, lo:hi] for lo, hi in zip(cuts, cuts[1:])]
    last = len(parts) - 1
    pieces = []
    for part in parts:
        pieces.append(along_lat(after(part, pieces[-1][2]) if pieces else part))
    sends = [sorted_rows(where, piece) for piece in pieces]
    kept = [along_lon(send) for send in sends]
    done = []
    for i in range(last):
        here = after(kept[i], sends[i + 1])
        got = [swapped(m, "lon", 1) for m in here]
        done.append(first_part(scalars, here, got, filt, rows))
    here = kept[last][:1] + after(kept[last][1:], *done)
    got = [swapped(m, "lon", 1) for m in here]
    result = last_part(scalars, here, got, filt, vert, done, rows, levels)
    return result.transpose(0, 1, 3, 2, 4)


def solution(mesh):
    placed = (P("lat", "lon", None, None), P(), P(), P(), P(), P())
    return jax.shard_map(
        on_device,
        mesh=mesh,
        in_specs=placed,
        out_specs=P("lat", "lon", None, None, None),
        check_vma=False,
    )
```

```python
import functools

import jax
import jax.numpy as jnp
from jax import lax
from jax.experimental import pallas as pl
from jax.experimental.pallas import tpu as pltpu
from jax.sharding import PartitionSpec as P

REACH = 3
SUBLANES = 16
LANES = 128
SPREAD_GAP = 8
CUTS = (48, 96)


SCALAR = pl.BlockSpec(memory_space=pltpu.SMEM)
PARAMS = pltpu.CompilerParams(vmem_limit_bytes=20 * 1024 * 1024)


def round_up(value, step):
    return (value + step - 1) // step * step


def band_of(slot_ref, slot):
    band = 0
    for i in range(slot_ref.shape[0]):
        band = jnp.where(slot_ref[i] == slot, i, band)
    return band


def table_kernel(where_ref, slot_ref, offset_ref, filter_ref, vertical_ref, filt_out, vert_out, lines):
    group, _, c, _ = filt_out.shape
    levels, bands, _ = vertical_ref.shape
    strips = [(lo, min(LANES, levels - lo)) for lo in range(0, levels, LANES)]
    for i, (lo, size) in enumerate(strips):
        strip = vertical_ref[:, :, lo : lo + size].astype(jnp.float32)
        lines[i, :, :size] = strip.reshape(levels * bands, size)
    filt_out[...] = jnp.zeros_like(filt_out)
    vert_out[...] = jnp.zeros_like(vert_out)
    for g in range(group):
        band = band_of(slot_ref, where_ref[1] * group + g)
        for k in range(filter_ref.shape[1]):
            n = offset_ref[band, k] + REACH
            for h in range(2):
                filt_out[g, n + h, :, h * c : (h + 1) * c] = filter_ref[band, k]
        for i, (lo, size) in enumerate(strips):
            strip = lines[i, pl.ds(band, levels, stride=bands), :]
            vert_out[g, :levels, lo : lo + size] = strip[:, :size].astype(vert_out.dtype)


def owned_tables(where, slot_of_band, block_offsets, filters, vertical, group, padded):
    c, levels = filters.shape[-1], vertical.shape[-1]
    vmem = pl.BlockSpec(memory_space=pltpu.VMEM)
    filt, vert = pl.pallas_call(
        table_kernel,
        in_specs=[SCALAR] * 3 + [vmem] * 2,
        out_specs=[vmem] * 2,
        out_shape=[
            jax.ShapeDtypeStruct((group, 2 * REACH + 2, c, 2 * c), filters.dtype),
            jax.ShapeDtypeStruct((group, padded, padded), vertical.dtype),
        ],
        scratch_shapes=[pltpu.VMEM((pl.cdiv(levels, LANES), vertical.shape[0] * levels, LANES), jnp.float32)],
        compiler_params=PARAMS,
        cost_estimate=pl.CostEstimate(flops=0, bytes_accessed=4000000, transcendentals=0),
    )(where, slot_of_band, block_offsets, filters, vertical.transpose(1, 0, 2))
    return filt.reshape(group, REACH + 1, 2 * c, 2 * c), vert


def row_weights(where_ref, slot_ref, weight_ref, r, b, rows, row_total):
    group = slot_ref.shape[0] // where_ref[3]
    band = band_of(slot_ref, where_ref[1] * group + b)
    row = where_ref[0] * rows + r
    above = jnp.where(row > 0, weight_ref[0, band], 0.0)
    below = jnp.where(row + 1 < row_total, weight_ref[2, band], 0.0)
    return above, weight_ref[1, band], below


def fill_window(window, place, weights, r, kept, got):
    chips = len(kept)
    shard_rows, per_source, _, c = kept[0].shape
    half = chips * per_source
    first = lax.rem(place, 2) * ((shard_rows - 2) // 2) + r

    def row_of(side, k, i, n):
        if side == 0:
            return kept[k][first + i, n]
        return got[0][k, r + i, n] if len(got) == 1 else got[k][first + i, n]

    for k in range(chips):
        for side in range(2):
            source = (place ^ (2 * k)) ^ side
            for n in range(per_source):
                value = None
                for i in range(3):
                    if side == 0:
                        row = kept[k][first + i, n]
                    elif len(got[0].shape) == 5:
                        row = got[0][k, r + i, n]
                    else:
                        row = got[k][first + i, n]
                    term = weights[i] * row.astype(jnp.float32)
                    value = term if value is None else value + term
                e = lax.rem(source * (per_source // 2) + (n + REACH) // 2, half)
                lane = (n + REACH) % 2 * c
                window[e, :, lane : lane + c] = value.astype(jnp.bfloat16)
    for e in range(window.shape[0] - half):
        window[half + e] = window[e]


def filtered(window, filt, j, step):
    _, depth, width = window.shape
    total = None
    for t in range(filt.shape[0]):
        lhs = window[j + t : j + t + step].reshape(step * depth, width)
        term = jnp.dot(lhs, filt[t], preferred_element_type=jnp.float32)
        total = term if total is None else total + term
    return total.astype(jnp.bfloat16)


def first_kernel(chips, where_ref, slot_ref, weight_ref, *refs):
    kept, got, (filt_ref, out_ref, window) = refs[:chips], refs[chips:-3], refs[-3:]
    r, b = pl.program_id(0), pl.program_id(1)
    rows = (kept[0].shape[0] - 2) // 2
    weights = row_weights(where_ref, slot_ref, weight_ref, r, b, rows, 2 * rows * chips)
    fill_window(window, where_ref[0], weights, r, kept, got)
    half, depth, width = out_ref.shape[2:]
    step = 4
    for j in range(0, half, step):
        out_ref[0, 0, j : j + step] = filtered(window, filt_ref[0], j, step).reshape(step, depth, width)


def last_kernel(chips, where_ref, slot_ref, weight_ref, *refs):
    kept, got, refs = refs[:chips], refs[chips : 2 * chips], refs[2 * chips :]
    filt_ref, vert_ref = refs[:2]
    done, (out_ref, window, spread) = refs[2:-3], refs[-3:]
    r, b = pl.program_id(0), pl.program_id(1)
    rows = (kept[0].shape[0] - 2) // 2
    weights = row_weights(where_ref, slot_ref, weight_ref, r, b, rows, 2 * rows * chips)
    fill_window(window, where_ref[0], weights, r, kept, got)
    levels, blocks, c = out_ref.shape[2:]
    half, depth = blocks // 2, window.shape[1]
    padded = vert_ref.shape[1]
    pitch = spread.shape[0] // padded
    step = 4
    for j in range(0, half, step):
        later = filtered(window, filt_ref[0], j, step)
        for i in range(step):
            column = [d[0, 0, j + i] for d in done] + [later[i * depth : (i + 1) * depth]]
            column = jnp.concatenate(column, axis=0)
            mixed = jnp.dot(vert_ref[0], column, preferred_element_type=jnp.float32)
            for h in range(2):
                spread[pl.ds(2 * (j + i) + h, padded, stride=pitch), :] = mixed[:, h * c : (h + 1) * c]
    for m in range(levels):
        out_ref[0, 0, m] = spread[m * pitch : m * pitch + blocks].astype(jnp.bfloat16)


def whole(a):
    return pl.BlockSpec(a.shape, lambda r, b: (0,) * a.ndim)


def banded(a):
    return pl.BlockSpec((1,) + a.shape[1:], lambda r, b: (b,) + (0,) * (a.ndim - 1))


def by_row_and_band(a):
    return pl.BlockSpec((1, 1) + a.shape[2:], lambda r, b: (b, r) + (0,) * (a.ndim - 2))


def first_part(scalars, kept, got, filt, rows):
    group, taps, width, _ = filt.shape
    _, per_source, depth, _ = kept[0].shape
    half = len(kept) * per_source
    out = jax.ShapeDtypeStruct((group, rows, half, depth, width), jnp.bfloat16)
    return pl.pallas_call(
        functools.partial(first_kernel, len(kept)),
        grid=(rows, group),
        in_specs=[SCALAR] * 3 + [whole(m) for m in kept + got] + [banded(filt)],
        out_specs=by_row_and_band(out),
        out_shape=out,
        scratch_shapes=[pltpu.VMEM((half + taps - 1, depth, width), jnp.bfloat16)],
        compiler_params=PARAMS,
        cost_estimate=pl.CostEstimate(flops=2000000000, bytes_accessed=8000000, transcendentals=0),
    )(*scalars, *kept, *got, filt)


def last_part(scalars, kept, got, filt, vert, done, rows, levels):
    group, taps, width, _ = filt.shape
    _, per_source, depth, c = kept[0].shape
    half = len(kept) * per_source
    padded = vert.shape[1]
    out = jax.ShapeDtypeStruct((group, rows, levels, 2 * half, c), jnp.bfloat16)
    return pl.pallas_call(
        functools.partial(last_kernel, len(kept)),
        grid=(rows, group),
        in_specs=[SCALAR] * 3
        + [whole(m) for m in kept + got]
        + [banded(filt), banded(vert)]
        + [by_row_and_band(d) for d in done],
        out_specs=by_row_and_band(out),
        out_shape=out,
        scratch_shapes=[
            pltpu.VMEM((half + taps - 1, depth, width), jnp.bfloat16),
            pltpu.VMEM((padded * (2 * half + SPREAD_GAP), c), jnp.float32),
        ],
        compiler_params=PARAMS,
        cost_estimate=pl.CostEstimate(flops=4_000_000_000, bytes_accessed=12_000_000, transcendentals=0),
    )(*scalars, *kept, *got, filt, vert, *done)


def swapped(value, axis, by):
    return lax.ppermute(value, axis, [(i, i ^ by) for i in range(lax.axis_size(axis))])


def sort_kernel(where_ref, *refs):
    count = (len(refs) - 1) // 2
    pieces, outs, sems = refs[:count], refs[count:-1], refs[-1]
    shard_rows = pieces[0].shape[0]
    chip, z = where_ref[0] // 2, where_ref[1]

    def copies(k, piece):
        main = pltpu.make_async_copy(piece, outs[k].at[pl.ds(1, shard_rows)], sems.at[k, 0])
        above = pltpu.make_async_copy(piece.at[pl.ds(shard_rows - 1, 1)], outs[k].at[pl.ds(0, 1)], sems.at[k, 1])
        below = pltpu.make_async_copy(piece.at[pl.ds(0, 1)], outs[k].at[pl.ds(shard_rows + 1, 1)], sems.at[k, 2])
        return main, above, below

    for k in range(count):
        plane = chip ^ k
        for j, piece in enumerate(pieces):
            main, above, below = copies(k, piece)
            pl.when((plane ^ z) == j)(main.start)
            pl.when((jnp.maximum(plane - 1, 0) ^ z) == j)(above.start)
            pl.when((jnp.minimum(plane + 1, count - 1) ^ z) == j)(below.start)
    for k in range(count):
        for copy in copies(k, pieces[0]):
            copy.wait()


def sorted_rows(where, pieces):
    shape = pieces[0].shape
    out = jax.ShapeDtypeStruct((shape[0] + 2,) + shape[1:], pieces[0].dtype)
    anywhere = pl.BlockSpec(memory_space=pl.ANY)
    return pl.pallas_call(
        sort_kernel,
        in_specs=[SCALAR] + [anywhere] * len(pieces),
        out_specs=[anywhere] * len(pieces),
        out_shape=[out] * len(pieces),
        scratch_shapes=[pltpu.SemaphoreType.DMA((len(pieces), 3))],
        compiler_params=PARAMS,
        cost_estimate=pl.CostEstimate(flops=0, bytes_accessed=3000000, transcendentals=0),
    )(where, *pieces)


def along_lat(own):
    pieces = {0: own}
    step = lax.axis_size("lat") // 2
    while step:
        pieces.update({j | step: swapped(piece, "lat", step) for j, piece in list(pieces.items())})
        step //= 2
    return [pieces[j] for j in range(len(pieces))]


def along_lon(sends):
    order = sorted(range(1, len(sends)), key=lambda k: -k)
    got = {k: swapped(sends[k], "lon", 2 * k) for k in order}
    return [sends[0]] + [got[k] for k in sorted(got)]


def give_kernel(where_ref, *refs):
    kept, (out_ref, sems) = refs[:-2], refs[-2:]
    count = out_ref.shape[1]
    first = (1 - where_ref[0] % 2) * (count - 2)
    copies = [
        pltpu.make_async_copy(m.at[pl.ds(first, count)], out_ref.at[k], sems.at[k]) for k, m in enumerate(kept)
    ]
    for copy in copies:
        copy.start()
    for copy in copies:
        copy.wait()


def given_rows(where, kept):
    shape = kept[0].shape
    anywhere = pl.BlockSpec(memory_space=pl.ANY)
    return pl.pallas_call(
        give_kernel,
        in_specs=[SCALAR] + [anywhere] * len(kept),
        out_specs=anywhere,
        out_shape=jax.ShapeDtypeStruct((len(kept), shape[0] // 2 + 1) + shape[1:], kept[0].dtype),
        scratch_shapes=[pltpu.SemaphoreType.DMA((len(kept),))],
        compiler_params=PARAMS,
        cost_estimate=pl.CostEstimate(flops=0, bytes_accessed=2_000_000, transcendentals=0),
    )(where, *kept)


def after(value, *marks):
    return lax.optimization_barrier((value, marks))[0]


def on_device(grad_field, lat_weights, block_offsets, filters, vertical, slot_of_band):
    shard_rows, _, levels, _ = grad_field.shape
    lats, lons = lax.axis_size("lat"), lax.axis_size("lon")
    rows = shard_rows * lats // lons
    group = slot_of_band.shape[0] // lats
    padded = round_up(levels, SUBLANES)
    extra = padded - levels
    cuts = [0] + list(CUTS) + [padded]

    place = [lax.axis_index("lon"), lax.axis_index("lat"), jnp.int32(lons), jnp.int32(lats)]
    where = jnp.stack(place).astype(jnp.int32)
    scalars = (where, slot_of_band, lat_weights.T)
    filt, vert = owned_tables(where, slot_of_band, block_offsets, filters, vertical, group, padded)

    own = jnp.pad(grad_field.astype(jnp.bfloat16), ((0, 0), (0, 0), (0, extra), (0, 0)))
    parts = [own[:, :, lo:hi] for lo, hi in zip(cuts, cuts[1:])]
    last = len(parts) - 1
    pieces = []
    for part in parts:
        pieces.append(along_lat(after(part, pieces[-1][2]) if pieces else part))
    sends = [sorted_rows(where, piece) for piece in pieces]
    kept = [along_lon(send) for send in sends]
    done = []
    for i in range(last):
        here = after(kept[i], sends[i + 1])
        got = [swapped(given_rows(where, here), "lon", 1)]
        done.append(first_part(scalars, here, got, filt, rows))
    here = kept[last][:1] + after(kept[last][1:], *done)
    got = [swapped(m, "lon", 1) for m in here]
    result = last_part(scalars, here, got, filt, vert, done, rows, levels)
    return result.transpose(0, 1, 3, 2, 4)


def solution(mesh):
    placed = (P("lat", "lon", None, None), P(), P(), P(), P(), P())
    return jax.shard_map(
        on_device,
        mesh=mesh,
        in_specs=placed,
        out_specs=P("lat", "lon", None, None, None),
        check_vma=False,
    )
```

```python
import functools

import jax
import jax.numpy as jnp
from jax import lax
from jax.experimental import pallas as pl
from jax.experimental.pallas import tpu as pltpu
from jax.sharding import PartitionSpec as P

REACH = 3
SUBLANES = 16
LANES = 128
SPREAD_GAP = 8
CUTS = (48, 96)


SCALAR = pl.BlockSpec(memory_space=pltpu.SMEM)
PARAMS = pltpu.CompilerParams(vmem_limit_bytes=20 * 1024 * 1024)


def round_up(value, step):
    return (value + step - 1) // step * step


def band_of(slot_ref, slot):
    band = 0
    for i in range(slot_ref.shape[0]):
        band = jnp.where(slot_ref[i] == slot, i, band)
    return band


def table_kernel(where_ref, slot_ref, offset_ref, filter_ref, vertical_ref, filt_out, vert_out, lines):
    group, _, c, _ = filt_out.shape
    levels, bands, _ = vertical_ref.shape
    strips = [(lo, min(LANES, levels - lo)) for lo in range(0, levels, LANES)]
    for i, (lo, size) in enumerate(strips):
        strip = vertical_ref[:, :, lo : lo + size].astype(jnp.float32)
        lines[i, :, :size] = strip.reshape(levels * bands, size)
    filt_out[...] = jnp.zeros_like(filt_out)
    vert_out[...] = jnp.zeros_like(vert_out)
    for g in range(group):
        band = band_of(slot_ref, where_ref[1] * group + g)
        for k in range(filter_ref.shape[1]):
            n = offset_ref[band, k] + REACH
            for h in range(2):
                filt_out[g, n + h, :, h * c : (h + 1) * c] = filter_ref[band, k]
        for i, (lo, size) in enumerate(strips):
            strip = lines[i, pl.ds(band, levels, stride=bands), :]
            vert_out[g, :levels, lo : lo + size] = strip[:, :size].astype(vert_out.dtype)


def owned_tables(where, slot_of_band, block_offsets, filters, vertical, group, padded):
    c, levels = filters.shape[-1], vertical.shape[-1]
    vmem = pl.BlockSpec(memory_space=pltpu.VMEM)
    filt, vert = pl.pallas_call(
        table_kernel,
        in_specs=[SCALAR] * 3 + [vmem] * 2,
        out_specs=[vmem] * 2,
        out_shape=[
            jax.ShapeDtypeStruct((group, 2 * REACH + 2, c, 2 * c), filters.dtype),
            jax.ShapeDtypeStruct((group, padded, padded), vertical.dtype),
        ],
        scratch_shapes=[pltpu.VMEM((pl.cdiv(levels, LANES), vertical.shape[0] * levels, LANES), jnp.float32)],
        compiler_params=PARAMS,
        cost_estimate=pl.CostEstimate(flops=0, bytes_accessed=4000000, transcendentals=0),
    )(where, slot_of_band, block_offsets, filters, vertical.transpose(1, 0, 2))
    return filt.reshape(group, REACH + 1, 2 * c, 2 * c), vert


def row_weights(where_ref, slot_ref, weight_ref, r, b, rows, row_total):
    group = slot_ref.shape[0] // where_ref[3]
    band = band_of(slot_ref, where_ref[1] * group + b)
    row = where_ref[0] * rows + r
    above = jnp.where(row > 0, weight_ref[0, band], 0.0)
    below = jnp.where(row + 1 < row_total, weight_ref[2, band], 0.0)
    return above, weight_ref[1, band], below


def fill_window(window, place, weights, r, kept, got):
    chips = len(kept)
    shard_rows, per_source, _, c = kept[0].shape
    half = chips * per_source
    first = lax.rem(place, 2) * ((shard_rows - 2) // 2) + r

    for k in range(chips):
        for side in range(2):
            source = (place ^ (2 * k)) ^ side
            for n in range(per_source):
                value = None
                for i in range(3):
                    if side == 0:
                        row = kept[k][first + i, n]
                    elif len(got[0].shape) == 5:
                        row = got[0][k, r + i, n]
                    else:
                        row = got[k][first + i, n]
                    term = weights[i] * row.astype(jnp.float32)
                    value = term if value is None else value + term
                e = lax.rem(source * (per_source // 2) + (n + REACH) // 2, half)
                lane = (n + REACH) % 2 * c
                window[e, :, lane : lane + c] = value.astype(jnp.bfloat16)
    for e in range(window.shape[0] - half):
        window[half + e] = window[e]


def filtered(window, filt, j, step):
    _, depth, width = window.shape
    total = None
    for t in range(filt.shape[0]):
        lhs = window[j + t : j + t + step].reshape(step * depth, width)
        term = jnp.dot(lhs, filt[t], preferred_element_type=jnp.float32)
        total = term if total is None else total + term
    return total.astype(jnp.bfloat16)


def first_kernel(chips, where_ref, slot_ref, weight_ref, *refs):
    kept, got, (filt_ref, out_ref, window) = refs[:chips], refs[chips:-3], refs[-3:]
    r, b = pl.program_id(0), pl.program_id(1)
    rows = (kept[0].shape[0] - 2) // 2
    weights = row_weights(where_ref, slot_ref, weight_ref, r, b, rows, 2 * rows * chips)
    fill_window(window, where_ref[0], weights, r, kept, got)
    half, depth, width = out_ref.shape[2:]
    step = 4
    for j in range(0, half, step):
        out_ref[0, 0, j : j + step] = filtered(window, filt_ref[0], j, step).reshape(step, depth, width)


def last_kernel(chips, where_ref, slot_ref, weight_ref, *refs):
    kept, got, refs = refs[:chips], refs[chips : 2 * chips], refs[2 * chips :]
    filt_ref, vert_ref = refs[:2]
    done, (out_ref, window, spread) = refs[2:-3], refs[-3:]
    r, b = pl.program_id(0), pl.program_id(1)
    rows = (kept[0].shape[0] - 2) // 2
    weights = row_weights(where_ref, slot_ref, weight_ref, r, b, rows, 2 * rows * chips)
    fill_window(window, where_ref[0], weights, r, kept, got)
    levels, blocks, c = out_ref.shape[2:]
    half, depth = blocks // 2, window.shape[1]
    padded = vert_ref.shape[1]
    pitch = spread.shape[0] // padded
    step = 4
    later = []
    for j in range(0, half, step):
        later.append(filtered(window, filt_ref[0], j, step))
    for j in range(half):
        here = later[j // step][j % step * depth : (j % step + 1) * depth]
        column = jnp.concatenate([d[0, 0, j] for d in done] + [here], axis=0)
        mixed = jnp.dot(vert_ref[0], column, preferred_element_type=jnp.float32)
        for h in range(2):
            spread[pl.ds(2 * j + h, padded, stride=pitch), :] = mixed[:, h * c : (h + 1) * c]
    for m in range(levels):
        out_ref[0, 0, m] = spread[m * pitch : m * pitch + blocks].astype(jnp.bfloat16)


def whole(a):
    return pl.BlockSpec(a.shape, lambda r, b: (0,) * a.ndim)


def banded(a):
    return pl.BlockSpec((1,) + a.shape[1:], lambda r, b: (b,) + (0,) * (a.ndim - 1))


def by_row_and_band(a):
    return pl.BlockSpec((1, 1) + a.shape[2:], lambda r, b: (b, r) + (0,) * (a.ndim - 2))


def first_part(scalars, kept, got, filt, rows):
    group, taps, width, _ = filt.shape
    _, per_source, depth, _ = kept[0].shape
    half = len(kept) * per_source
    out = jax.ShapeDtypeStruct((group, rows, half, depth, width), jnp.bfloat16)
    return pl.pallas_call(
        functools.partial(first_kernel, len(kept)),
        grid=(rows, group),
        in_specs=[SCALAR] * 3 + [whole(m) for m in kept + got] + [banded(filt)],
        out_specs=by_row_and_band(out),
        out_shape=out,
        scratch_shapes=[pltpu.VMEM((half + taps - 1, depth, width), jnp.bfloat16)],
        compiler_params=PARAMS,
        cost_estimate=pl.CostEstimate(flops=2000000000, bytes_accessed=8000000, transcendentals=0),
    )(*scalars, *kept, *got, filt)


def last_part(scalars, kept, got, filt, vert, done, rows, levels):
    group, taps, width, _ = filt.shape
    _, per_source, depth, c = kept[0].shape
    half = len(kept) * per_source
    padded = vert.shape[1]
    out = jax.ShapeDtypeStruct((group, rows, levels, 2 * half, c), jnp.bfloat16)
    return pl.pallas_call(
        functools.partial(last_kernel, len(kept)),
        grid=(rows, group),
        in_specs=[SCALAR] * 3
        + [whole(m) for m in kept + got]
        + [banded(filt), banded(vert)]
        + [by_row_and_band(d) for d in done],
        out_specs=by_row_and_band(out),
        out_shape=out,
        scratch_shapes=[
            pltpu.VMEM((half + taps - 1, depth, width), jnp.bfloat16),
            pltpu.VMEM((padded * (2 * half + SPREAD_GAP), c), jnp.float32),
        ],
        compiler_params=PARAMS,
        cost_estimate=pl.CostEstimate(flops=4_000_000_000, bytes_accessed=12_000_000, transcendentals=0),
    )(*scalars, *kept, *got, filt, vert, *done)


def swapped(value, axis, by):
    return lax.ppermute(value, axis, [(i, i ^ by) for i in range(lax.axis_size(axis))])


def sort_kernel(where_ref, *refs):
    count = (len(refs) - 1) // 2
    pieces, outs, sems = refs[:count], refs[count:-1], refs[-1]
    shard_rows = pieces[0].shape[0]
    chip, z = where_ref[0] // 2, where_ref[1]

    def copies(k, piece):
        main = pltpu.make_async_copy(piece, outs[k].at[pl.ds(1, shard_rows)], sems.at[k, 0])
        above = pltpu.make_async_copy(piece.at[pl.ds(shard_rows - 1, 1)], outs[k].at[pl.ds(0, 1)], sems.at[k, 1])
        below = pltpu.make_async_copy(piece.at[pl.ds(0, 1)], outs[k].at[pl.ds(shard_rows + 1, 1)], sems.at[k, 2])
        return main, above, below

    for k in range(count):
        plane = chip ^ k
        for j, piece in enumerate(pieces):
            main, above, below = copies(k, piece)
            pl.when((plane ^ z) == j)(main.start)
            pl.when((jnp.maximum(plane - 1, 0) ^ z) == j)(above.start)
            pl.when((jnp.minimum(plane + 1, count - 1) ^ z) == j)(below.start)
    for k in range(count):
        for copy in copies(k, pieces[0]):
            copy.wait()


def sorted_rows(where, pieces):
    shape = pieces[0].shape
    out = jax.ShapeDtypeStruct((shape[0] + 2,) + shape[1:], pieces[0].dtype)
    anywhere = pl.BlockSpec(memory_space=pl.ANY)
    return pl.pallas_call(
        sort_kernel,
        in_specs=[SCALAR] + [anywhere] * len(pieces),
        out_specs=[anywhere] * len(pieces),
        out_shape=[out] * len(pieces),
        scratch_shapes=[pltpu.SemaphoreType.DMA((len(pieces), 3))],
        compiler_params=PARAMS,
        cost_estimate=pl.CostEstimate(flops=0, bytes_accessed=3000000, transcendentals=0),
    )(where, *pieces)


def along_lat(own):
    pieces = {0: own}
    step = lax.axis_size("lat") // 2
    while step:
        pieces.update({j | step: swapped(piece, "lat", step) for j, piece in list(pieces.items())})
        step //= 2
    return [pieces[j] for j in range(len(pieces))]


def along_lon(sends):
    order = sorted(range(1, len(sends)), key=lambda k: -k)
    got = {k: swapped(sends[k], "lon", 2 * k) for k in order}
    return [sends[0]] + [got[k] for k in sorted(got)]


def give_kernel(where_ref, *refs):
    kept, (out_ref, sems) = refs[:-2], refs[-2:]
    count = out_ref.shape[1]
    first = (1 - where_ref[0] % 2) * (count - 2)
    copies = [
        pltpu.make_async_copy(m.at[pl.ds(first, count)], out_ref.at[k], sems.at[k]) for k, m in enumerate(kept)
    ]
    for copy in copies:
        copy.start()
    for copy in copies:
        copy.wait()


def given_rows(where, kept):
    shape = kept[0].shape
    anywhere = pl.BlockSpec(memory_space=pl.ANY)
    return pl.pallas_call(
        give_kernel,
        in_specs=[SCALAR] + [anywhere] * len(kept),
        out_specs=anywhere,
        out_shape=jax.ShapeDtypeStruct((len(kept), shape[0] // 2 + 1) + shape[1:], kept[0].dtype),
        scratch_shapes=[pltpu.SemaphoreType.DMA((len(kept),))],
        compiler_params=PARAMS,
        cost_estimate=pl.CostEstimate(flops=0, bytes_accessed=2_000_000, transcendentals=0),
    )(where, *kept)


def after(value, *marks):
    return lax.optimization_barrier((value, marks))[0]


def on_device(grad_field, lat_weights, block_offsets, filters, vertical, slot_of_band):
    shard_rows, _, levels, _ = grad_field.shape
    lats, lons = lax.axis_size("lat"), lax.axis_size("lon")
    rows = shard_rows * lats // lons
    group = slot_of_band.shape[0] // lats
    padded = round_up(levels, SUBLANES)
    extra = padded - levels
    cuts = [0] + list(CUTS) + [padded]

    place = [lax.axis_index("lon"), lax.axis_index("lat"), jnp.int32(lons), jnp.int32(lats)]
    where = jnp.stack(place).astype(jnp.int32)
    scalars = (where, slot_of_band, lat_weights.T)
    filt, vert = owned_tables(where, slot_of_band, block_offsets, filters, vertical, group, padded)

    own = jnp.pad(grad_field.astype(jnp.bfloat16), ((0, 0), (0, 0), (0, extra), (0, 0)))
    parts = [own[:, :, lo:hi] for lo, hi in zip(cuts, cuts[1:])]
    last = len(parts) - 1
    pieces = []
    for part in parts:
        pieces.append(along_lat(after(part, pieces[-1][2]) if pieces else part))
    pieces[0], filt, vert = lax.optimization_barrier((pieces[0], filt, vert))
    sends = [sorted_rows(where, piece) for piece in pieces]
    kept = [along_lon(send) for send in sends]
    done = []
    for i in range(last):
        here = after(kept[i], sends[i + 1])
        got = [swapped(given_rows(where, here), "lon", 1)]
        done.append(first_part(scalars, here, got, filt, rows))
    here = kept[last][:1] + after(kept[last][1:], *done)
    got = [swapped(m, "lon", 1) for m in here]
    result = last_part(scalars, here, got, filt, vert, done, rows, levels)
    return result.transpose(0, 1, 3, 2, 4)


def solution(mesh):
    placed = (P("lat", "lon", None, None), P(), P(), P(), P(), P())
    return jax.shard_map(
        on_device,
        mesh=mesh,
        in_specs=placed,
        out_specs=P("lat", "lon", None, None, None),
        check_vma=False,
    )
```

```python
import functools

import jax
import jax.numpy as jnp
from jax import lax
from jax.experimental import pallas as pl
from jax.experimental.pallas import tpu as pltpu
from jax.sharding import PartitionSpec as P

REACH = 3
SUBLANES = 16
LANES = 128
SPREAD_GAP = 8
CUTS = (48, 96)


SCALAR = pl.BlockSpec(memory_space=pltpu.SMEM)
PARAMS = pltpu.CompilerParams(vmem_limit_bytes=20 * 1024 * 1024)


def round_up(value, step):
    return (value + step - 1) // step * step


def band_of(slot_ref, slot):
    band = 0
    for i in range(slot_ref.shape[0]):
        band = jnp.where(slot_ref[i] == slot, i, band)
    return band


def table_kernel(where_ref, slot_ref, offset_ref, filter_ref, vertical_ref, filt_out, vert_out, lines):
    group, _, c, _ = filt_out.shape
    levels, bands, _ = vertical_ref.shape
    strips = [(lo, min(LANES, levels - lo)) for lo in range(0, levels, LANES)]
    for i, (lo, size) in enumerate(strips):
        strip = vertical_ref[:, :, lo : lo + size].astype(jnp.float32)
        lines[i, :, :size] = strip.reshape(levels * bands, size)
    filt_out[...] = jnp.zeros_like(filt_out)
    vert_out[...] = jnp.zeros_like(vert_out)
    for g in range(group):
        band = band_of(slot_ref, where_ref[1] * group + g)
        for k in range(filter_ref.shape[1]):
            n = offset_ref[band, k] + REACH
            for h in range(2):
                filt_out[g, n + h, :, h * c : (h + 1) * c] = filter_ref[band, k]
        for i, (lo, size) in enumerate(strips):
            strip = lines[i, pl.ds(band, levels, stride=bands), :]
            vert_out[g, :levels, lo : lo + size] = strip[:, :size].astype(vert_out.dtype)


def owned_tables(where, slot_of_band, block_offsets, filters, vertical, group, padded):
    c, levels = filters.shape[-1], vertical.shape[-1]
    vmem = pl.BlockSpec(memory_space=pltpu.VMEM)
    filt, vert = pl.pallas_call(
        table_kernel,
        in_specs=[SCALAR] * 3 + [vmem] * 2,
        out_specs=[vmem] * 2,
        out_shape=[
            jax.ShapeDtypeStruct((group, 2 * REACH + 2, c, 2 * c), filters.dtype),
            jax.ShapeDtypeStruct((group, padded, padded), vertical.dtype),
        ],
        scratch_shapes=[pltpu.VMEM((pl.cdiv(levels, LANES), vertical.shape[0] * levels, LANES), jnp.float32)],
        compiler_params=PARAMS,
        cost_estimate=pl.CostEstimate(flops=0, bytes_accessed=4000000, transcendentals=0),
    )(where, slot_of_band, block_offsets, filters, vertical.transpose(1, 0, 2))
    return filt.reshape(group, REACH + 1, 2 * c, 2 * c), vert


def row_weights(where_ref, slot_ref, weight_ref, r, b, rows, row_total):
    group = slot_ref.shape[0] // where_ref[3]
    band = band_of(slot_ref, where_ref[1] * group + b)
    row = where_ref[0] * rows + r
    above = jnp.where(row > 0, weight_ref[0, band], 0.0)
    below = jnp.where(row + 1 < row_total, weight_ref[2, band], 0.0)
    return above, weight_ref[1, band], below


def fill_window(window, place, weights, r, kept, got):
    chips = len(kept)
    shard_rows, per_source, _, c = kept[0].shape
    half = chips * per_source
    first = lax.rem(place, 2) * ((shard_rows - 2) // 2) + r

    for k in range(chips):
        for side in range(2):
            source = (place ^ (2 * k)) ^ side
            for n in range(per_source):
                value = None
                for i in range(3):
                    if side == 0:
                        row = kept[k][first + i, n]
                    elif len(got[0].shape) == 5:
                        row = got[0][k, r + i, n]
                    else:
                        row = got[k][first + i, n]
                    term = weights[i] * row.astype(jnp.float32)
                    value = term if value is None else value + term
                e = lax.rem(source * (per_source // 2) + (n + REACH) // 2, half)
                lane = (n + REACH) % 2 * c
                window[e, :, lane : lane + c] = value.astype(jnp.bfloat16)
    for e in range(window.shape[0] - half):
        window[half + e] = window[e]


def filtered(window, filt, j, step):
    _, depth, width = window.shape
    total = None
    for t in range(filt.shape[0]):
        lhs = window[j + t : j + t + step].reshape(step * depth, width)
        term = jnp.dot(lhs, filt[t], preferred_element_type=jnp.float32)
        total = term if total is None else total + term
    return total.astype(jnp.bfloat16)


def first_kernel(chips, where_ref, slot_ref, weight_ref, *refs):
    kept, got, (filt_ref, out_ref, window) = refs[:chips], refs[chips:-3], refs[-3:]
    r, b = pl.program_id(0), pl.program_id(1)
    rows = (kept[0].shape[0] - 2) // 2
    weights = row_weights(where_ref, slot_ref, weight_ref, r, b, rows, 2 * rows * chips)
    fill_window(window, where_ref[0], weights, r, kept, got)
    half, depth, width = out_ref.shape[2:]
    step = 4
    for j in range(0, half, step):
        out_ref[0, 0, j : j + step] = filtered(window, filt_ref[0], j, step).reshape(step, depth, width)


def last_kernel(chips, where_ref, slot_ref, weight_ref, *refs):
    kept, got, refs = refs[:chips], refs[chips : 2 * chips], refs[2 * chips :]
    filt_ref, vert_ref = refs[:2]
    done, (out_ref, window, spread) = refs[2:-3], refs[-3:]
    r, b = pl.program_id(0), pl.program_id(1)
    rows = (kept[0].shape[0] - 2) // 2
    weights = row_weights(where_ref, slot_ref, weight_ref, r, b, rows, 2 * rows * chips)
    fill_window(window, where_ref[0], weights, r, kept, got)
    levels, blocks, c = out_ref.shape[2:]
    half, depth = blocks // 2, window.shape[1]
    padded = vert_ref.shape[1]
    pitch = spread.shape[0] // padded
    step = 4
    later = []
    for j in range(0, half, step):
        later.append(filtered(window, filt_ref[0], j, step))
    for j in range(half):
        here = later[j // step][j % step * depth : (j % step + 1) * depth]
        column = jnp.concatenate([d[0, 0, j] for d in done] + [here], axis=0)
        mixed = jnp.dot(vert_ref[0], column, preferred_element_type=jnp.float32)
        for h in range(2):
            spread[pl.ds(2 * j + h, padded, stride=pitch), :] = mixed[:, h * c : (h + 1) * c]
    for m in range(levels):
        out_ref[0, 0, m] = spread[m * pitch : m * pitch + blocks].astype(jnp.bfloat16)


def whole(a):
    return pl.BlockSpec(a.shape, lambda r, b: (0,) * a.ndim)


def banded(a):
    return pl.BlockSpec((1,) + a.shape[1:], lambda r, b: (b,) + (0,) * (a.ndim - 1))


def by_row_and_band(a):
    return pl.BlockSpec((1, 1) + a.shape[2:], lambda r, b: (b, r) + (0,) * (a.ndim - 2))


def first_part(scalars, kept, got, filt, rows):
    group, taps, width, _ = filt.shape
    _, per_source, depth, _ = kept[0].shape
    half = len(kept) * per_source
    out = jax.ShapeDtypeStruct((group, rows, half, depth, width), jnp.bfloat16)
    return pl.pallas_call(
        functools.partial(first_kernel, len(kept)),
        grid=(rows, group),
        in_specs=[SCALAR] * 3 + [whole(m) for m in kept + got] + [banded(filt)],
        out_specs=by_row_and_band(out),
        out_shape=out,
        scratch_shapes=[pltpu.VMEM((half + taps - 1, depth, width), jnp.bfloat16)],
        compiler_params=PARAMS,
        cost_estimate=pl.CostEstimate(flops=2000000000, bytes_accessed=8000000, transcendentals=0),
    )(*scalars, *kept, *got, filt)


def last_part(scalars, kept, got, filt, vert, done, rows, levels):
    group, taps, width, _ = filt.shape
    _, per_source, depth, c = kept[0].shape
    half = len(kept) * per_source
    padded = vert.shape[1]
    out = jax.ShapeDtypeStruct((group, rows, levels, 2 * half, c), jnp.bfloat16)
    return pl.pallas_call(
        functools.partial(last_kernel, len(kept)),
        grid=(rows, group),
        in_specs=[SCALAR] * 3
        + [whole(m) for m in kept + got]
        + [banded(filt), banded(vert)]
        + [by_row_and_band(d) for d in done],
        out_specs=by_row_and_band(out),
        out_shape=out,
        scratch_shapes=[
            pltpu.VMEM((half + taps - 1, depth, width), jnp.bfloat16),
            pltpu.VMEM((padded * (2 * half + SPREAD_GAP), c), jnp.float32),
        ],
        compiler_params=PARAMS,
        cost_estimate=pl.CostEstimate(flops=4_000_000_000, bytes_accessed=12_000_000, transcendentals=0),
    )(*scalars, *kept, *got, filt, vert, *done)


def swapped(value, axis, by):
    return lax.ppermute(value, axis, [(i, i ^ by) for i in range(lax.axis_size(axis))])


def sort_kernel(where_ref, *refs):
    count = len(refs) // 2
    pieces, outs = refs[:count], refs[count:]
    shard_rows = pieces[0].shape[0]
    chip, z = where_ref[0] // 2, where_ref[1]

    def lay(out, first, piece, row, length):
        out[first : first + length] = piece[row : row + length]

    for k, out in enumerate(outs):
        plane = chip ^ k
        for j, piece in enumerate(pieces):
            below, above = jnp.maximum(plane - 1, 0), jnp.minimum(plane + 1, count - 1)
            pl.when((plane ^ z) == j)(functools.partial(lay, out, 1, piece, 0, shard_rows))
            pl.when((below ^ z) == j)(functools.partial(lay, out, 0, piece, shard_rows - 1, 1))
            pl.when((above ^ z) == j)(functools.partial(lay, out, shard_rows + 1, piece, 0, 1))


def sorted_rows(where, pieces):
    shape = pieces[0].shape
    out = jax.ShapeDtypeStruct((shape[0] + 2,) + shape[1:], pieces[0].dtype)
    vmem = pl.BlockSpec(memory_space=pltpu.VMEM)
    return pl.pallas_call(
        sort_kernel,
        in_specs=[SCALAR] + [vmem] * len(pieces),
        out_specs=[vmem] * len(pieces),
        out_shape=[out] * len(pieces),
        compiler_params=PARAMS,
        cost_estimate=pl.CostEstimate(flops=0, bytes_accessed=3000000, transcendentals=0),
    )(where, *pieces)


def along_lat(own):
    pieces = {0: own}
    step = lax.axis_size("lat") // 2
    while step:
        pieces.update({j | step: swapped(piece, "lat", step) for j, piece in list(pieces.items())})
        step //= 2
    return [pieces[j] for j in range(len(pieces))]


def along_lon(sends):
    order = sorted(range(1, len(sends)), key=lambda k: -k)
    got = {k: swapped(sends[k], "lon", 2 * k) for k in order}
    return [sends[0]] + [got[k] for k in sorted(got)]


def give_kernel(where_ref, *refs):
    kept, out_ref = refs[:-1], refs[-1]
    count = out_ref.shape[1]
    first = (1 - where_ref[0] % 2) * (count - 2)
    for k, m in enumerate(kept):
        out_ref[k] = m[pl.ds(first, count)]


def given_rows(where, kept):
    shape = kept[0].shape
    vmem = pl.BlockSpec(memory_space=pltpu.VMEM)
    return pl.pallas_call(
        give_kernel,
        in_specs=[SCALAR] + [vmem] * len(kept),
        out_specs=vmem,
        out_shape=jax.ShapeDtypeStruct((len(kept), shape[0] // 2 + 1) + shape[1:], kept[0].dtype),
        compiler_params=PARAMS,
        cost_estimate=pl.CostEstimate(flops=0, bytes_accessed=2_000_000, transcendentals=0),
    )(where, *kept)


def after(value, *marks):
    return lax.optimization_barrier((value, marks))[0]


def on_device(grad_field, lat_weights, block_offsets, filters, vertical, slot_of_band):
    shard_rows, _, levels, _ = grad_field.shape
    lats, lons = lax.axis_size("lat"), lax.axis_size("lon")
    rows = shard_rows * lats // lons
    group = slot_of_band.shape[0] // lats
    padded = round_up(levels, SUBLANES)
    extra = padded - levels
    cuts = [0] + list(CUTS) + [padded]

    place = [lax.axis_index("lon"), lax.axis_index("lat"), jnp.int32(lons), jnp.int32(lats)]
    where = jnp.stack(place).astype(jnp.int32)
    scalars = (where, slot_of_band, lat_weights.T)
    filt, vert = owned_tables(where, slot_of_band, block_offsets, filters, vertical, group, padded)

    own = jnp.pad(grad_field.astype(jnp.bfloat16), ((0, 0), (0, 0), (0, extra), (0, 0)))
    parts = [own[:, :, lo:hi] for lo, hi in zip(cuts, cuts[1:])]
    last = len(parts) - 1
    pieces = []
    for part in parts:
        pieces.append(along_lat(after(part, pieces[-1][2]) if pieces else part))
    pieces[0], filt, vert = lax.optimization_barrier((pieces[0], filt, vert))
    sends = [sorted_rows(where, piece) for piece in pieces]
    kept = [along_lon(send) for send in sends]
    done = []
    for i in range(last):
        here = after(kept[i], sends[i + 1])
        got = [swapped(given_rows(where, here), "lon", 1)]
        done.append(first_part(scalars, here, got, filt, rows))
    here = kept[last][:1] + after(kept[last][1:], *done)
    got = [swapped(m, "lon", 1) for m in here]
    result = last_part(scalars, here, got, filt, vert, done, rows, levels)
    return result.transpose(0, 1, 3, 2, 4)


def solution(mesh):
    placed = (P("lat", "lon", None, None), P(), P(), P(), P(), P())
    return jax.shard_map(
        on_device,
        mesh=mesh,
        in_specs=placed,
        out_specs=P("lat", "lon", None, None, None),
        check_vma=False,
    )
```
